256 devices in a mesh: group: 16 (over z_hi, x), mp: 16 (over y, z_lo, core).
Axes of the slice: x: 4, y: 4, z: 8 (z_hi: 4, z_lo: 2; z = z_hi * 2 + z_lo), core: 2. Of those that a mesh axis runs over, the one named last changes fastest.
Arguments:
- activations: bfloat16 [32, 18432], P('group', 'mp'), may hold values from -8 to 8
- qkv_values: bfloat16 [18432, 5376], P('mp', 'group'), may hold values from -4 to 4
- qkv_scales: float32 [144, 42], P('mp'), may hold values from 0.0036828478 to 0.014731391
- block_order: int32 [42], replicated, may hold values from 0 to 41, as said below
- out_values: bfloat16 [4608, 18432], P('group', 'mp'), may hold values from -4 to 4
- out_scales: float32 [36, 144], P(None, 'mp'), may hold values from 0.0073656957 to 0.029462783
- kv_cache: bfloat16 [32, 32768, 768], P('group', 'mp'), may hold values from -8 to 8
- cache_len: int32 [32], P('group'), may hold values from 4096 to 32768, as said below
Outputs:
- attn_out: bfloat16 [32, 18432], P('group', 'mp')
The draws below stay inside these ranges and needn't reach their ends.
Inputs may be any that keep to these rules, and one draw needn't show every extreme that they name: `cache_len`: each row's count of valid cached positions; some row has all 32768. `block_order`: a permutation of the logical column blocks.
All inputs are finite; a program needn't handle non-finite values.
Results may differ from the reference program's by a relative error of at most 0.034.
Values may be sent and summed in bfloat16 or wider, within the bound.
No kernel may reach another device: no remote copies, remote signals or barrier semaphores. Data moves between devices by JAX's collectives and lax.ppermute only.
A program may use at most 128 MiB of HBM per device.

```python
import math
import jax
import jax.numpy as jnp
from jax import lax

D = 18432
HD = 192
QH = 12
KVH = 2
BLK = 128
QW = 4608
QKVW = 5376
LENGTH = 32768
ROWS_ALL = 32


def rotate_pairs(vectors, position):
    half_width = vectors.shape[-1] // 2
    frequency = 10000.0 ** (-jnp.arange(half_width, dtype=jnp.float32) / half_width)
    angles = position[..., None] * frequency
    cos_part = jnp.cos(angles)
    sin_part = jnp.sin(angles)
    first_half = vectors[..., :half_width]
    second_half = vectors[..., half_width:]
    return jnp.concatenate([first_half * cos_part - second_half * sin_part, first_half * sin_part + second_half * cos_part], axis=-1)


def shared_layout(key):
    subkeys = jax.random.split(key, 10)
    feature_signs = jnp.where(jax.random.randint(subkeys[0], (D,), 0, 2) == 0, -1.0, 1.0).astype(jnp.float32)
    pattern = jnp.where(jax.random.randint(subkeys[1], (HD,), 0, 2) == 0, -1.0, 1.0).astype(jnp.float32)
    block_perm = jax.random.permutation(subkeys[2], QKVW // BLK).astype(jnp.int32)
    lengths = jax.random.randint(subkeys[3], (ROWS_ALL,), LENGTH // 8, LENGTH + 1)
    full_row = jax.random.randint(subkeys[4], (), 0, ROWS_ALL)
    lengths = lengths.at[full_row].set(LENGTH).astype(jnp.int32)
    levels = jax.random.randint(subkeys[5], (ROWS_ALL,), 0, 4)
    strong_row = jax.random.randint(subkeys[6], (), 0, ROWS_ALL)
    weak_row = (strong_row + 1 + jax.random.randint(subkeys[7], (), 0, ROWS_ALL - 1)) % ROWS_ALL
    levels = levels.at[strong_row].set(3).at[weak_row].set(0).astype(jnp.int32)
    first_pos = jax.random.randint(subkeys[8], (ROWS_ALL,), 0, lengths)
    offset = 1 + jax.random.randint(subkeys[9], (ROWS_ALL,), 0, lengths - 1)
    second_pos = (first_pos + offset) % lengths
    return (feature_signs, pattern, block_perm, lengths, levels, first_pos.astype(jnp.int32), second_pos.astype(jnp.int32))


def draw_activations(key, part):
    feature_signs, pattern, block_perm, lengths, levels, first_pos, second_pos = shared_layout(key)
    key = jax.random.fold_in(key, 3)
    jitter = jnp.clip(2.0 * jax.random.normal(key, (ROWS_ALL, D), jnp.float32), -8.0, 8.0)
    target = 280.0
    strength = levels.astype(jnp.float32) / 3.0 * target / (4.0 * HD ** 0.5) / 7.36
    return jnp.clip(jitter + strength[:, None] * feature_signs[None, :], -8.0, 8.0).astype(jnp.bfloat16)


def draw_qkv_values(key, part):
    feature_signs, pattern, block_perm, lengths, levels, first_pos, second_pos = shared_layout(key)
    key = jax.random.fold_in(key, 5)
    jitter = jnp.clip(jax.random.normal(key, (D, QKVW), jnp.float32), -4.0, 4.0)
    stored_cols = jnp.arange(QKVW)
    logical = block_perm[stored_cols // BLK] * BLK + stored_cols % BLK
    coherent = jnp.where(logical < QW, pattern[logical % HD], 0.0)
    weight = 6.8 / D ** 0.5
    return jnp.clip(jitter + weight * feature_signs[:, None] * coherent[None, :], -4.0, 4.0).astype(jnp.bfloat16)


def draw_block_order(key, part):
    feature_signs, pattern, block_perm, lengths, levels, first_pos, second_pos = shared_layout(key)
    return block_perm


def draw_cache_len(key, part):
    feature_signs, pattern, block_perm, lengths, levels, first_pos, second_pos = shared_layout(key)
    return lengths


def draw_kv_cache(key, part):
    feature_signs, pattern, block_perm, lengths, levels, first_pos, second_pos = shared_layout(key)
    key = jax.random.fold_in(key, 11)
    whole_cache = jnp.clip(2.0 * jax.random.normal(key, (ROWS_ALL, LENGTH, 2 * KVH * HD), jnp.float32), -8.0, 8.0)
    planted = 4.0 * rotate_pairs(jnp.broadcast_to(pattern, (ROWS_ALL, HD)), lengths.astype(jnp.float32))
    planted = jnp.tile(planted, (1, KVH))
    row_ids = jnp.arange(ROWS_ALL)
    whole_cache = whole_cache.at[row_ids, first_pos, :KVH * HD].set(planted)
    whole_cache = whole_cache.at[row_ids, second_pos, :KVH * HD].set(planted * 0.992)
    return whole_cache.astype(jnp.bfloat16)


def block_levels(key, extent, cuts, smallest, largest):
    def one(dim, blocks):
        heights = jax.random.uniform(jax.random.fold_in(jax.random.fold_in(key, 6), dim), (blocks,), jnp.float32, smallest / len(cuts), largest / len(cuts))
        return jnp.repeat(jnp.exp(heights), extent[dim] // blocks).reshape((-1,) + (1,) * (len(extent) - dim - 1))

    factor_of = one(*cuts[0])
    for cut in cuts[1:]:
        factor_of = factor_of * one(*cut)
    return factor_of


def bell_draw(stream_key, dims, deviation, most, cuts=(), kind=jnp.bfloat16):
    loudness = block_levels(stream_key, dims, cuts, -0.22, 0.18) if cuts else 1.0
    result = jax.random.normal(stream_key, dims, jnp.float32) * deviation * loudness
    return jnp.minimum(jnp.maximum(result, -most), most).astype(kind)


def setup_inputs(seed: int = 0) -> dict:
    arg_keys = jax.random.split(jax.random.key(seed), 9)
    return {
        "activations": draw_activations(jax.random.fold_in(arg_keys[8], 71), 0),
        "qkv_values": draw_qkv_values(jax.random.fold_in(arg_keys[8], 71), 0),
        "qkv_scales": jnp.clip(jnp.exp(math.log(0.014731391) - 1.3862944 * jax.random.uniform(arg_keys[2], (D // BLK, QKVW // BLK), jnp.float32) ** block_levels(arg_keys[2], (D // BLK, QKVW // BLK), ((0, 16),), -0.2, 0.2)), 0.0036828478, 0.014731391),
        "block_order": draw_block_order(jax.random.fold_in(arg_keys[8], 71), 0),
        "out_values": bell_draw(arg_keys[4], (QW, D), 1.0, 4.0, ((0, 16), (1, 16))),
        "out_scales": jnp.clip(jnp.exp(math.log(0.029462783) - 1.3862944 * jax.random.uniform(arg_keys[5], (QW // BLK, D // BLK), jnp.float32) ** block_levels(arg_keys[5], (QW // BLK, D // BLK), ((1, 16),), -0.2, 0.2)), 0.0073656957, 0.029462783),
        "kv_cache": draw_kv_cache(jax.random.fold_in(arg_keys[8], 71), 0),
        "cache_len": draw_cache_len(jax.random.fold_in(arg_keys[8], 71), 0),
    }


def rotate(vec, pos):
    half = vec.shape[-1] // 2
    freq = 10000.0 ** (-jnp.arange(half, dtype=jnp.float32) / half)
    angle = pos[..., None] * freq
    cosine = jnp.cos(angle)
    sine = jnp.sin(angle)
    first = vec[..., :half]
    second = vec[..., half:]
    return jnp.concatenate([first * cosine - second * sine, first * sine + second * cosine], axis=-1)


def reference(activations, qkv_values, qkv_scales, block_order, out_values, out_scales, kv_cache, cache_len):
    nblk = QKVW // BLK
    kvw = KVH * HD
    scale_cols = qkv_scales[:, block_order]
    qkv_weight = (qkv_values.astype(jnp.float32).reshape(D // BLK, BLK, nblk, BLK) * scale_cols[:, None, :, None]).reshape(D, QKVW).astype(jnp.bfloat16)
    stored = jnp.dot(activations, qkv_weight, preferred_element_type=jnp.float32)
    blocks = stored.reshape(ROWS_ALL, nblk, BLK)
    qkv = jnp.zeros_like(blocks).at[:, block_order].set(blocks).reshape(ROWS_ALL, QKVW)
    pos = cache_len.astype(jnp.float32)
    q_rot = rotate(qkv[:, :QW].reshape(ROWS_ALL, KVH, QH, HD), pos[:, None, None]).astype(jnp.bfloat16)
    k_new = rotate(qkv[:, QW:QW + kvw].reshape(ROWS_ALL, KVH, HD), pos[:, None]).astype(jnp.bfloat16)
    v_new = qkv[:, QW + kvw:].reshape(ROWS_ALL, KVH, HD).astype(jnp.bfloat16)
    factor = HD ** -0.5

    def one_row(items):
        query, cache, length, key_new, val_new = items
        valid = jnp.arange(LENGTH) < length
        keys = cache[:, :kvw].reshape(LENGTH, KVH, HD).astype(jnp.float32)
        vals = cache[:, kvw:].reshape(LENGTH, KVH, HD).astype(jnp.float32)
        query32 = query.astype(jnp.float32)
        scores = jnp.einsum("gqd,tgd->gqt", query32, keys) * factor
        scores = jnp.where(valid[None, None, :], scores, -1e30)
        s_new = jnp.sum(query32 * key_new.astype(jnp.float32)[:, None, :], axis=-1) * factor
        top = jnp.maximum(jnp.max(scores, axis=-1), s_new)
        expo = jnp.exp(scores - top[..., None]) * valid[None, None, :].astype(jnp.float32)
        own = jnp.exp(s_new - top)
        total = jnp.sum(expo, axis=-1) + own
        weights = expo.astype(jnp.bfloat16)
        numer = jnp.einsum("gqt,tgd->gqd", weights.astype(jnp.float32), vals)
        numer = numer + own[..., None] * val_new.astype(jnp.float32)[:, None, :]
        return (numer / total[..., None]).astype(jnp.bfloat16)

    heads_out = lax.map(one_row, (q_rot, kv_cache, cache_len, k_new, v_new)).reshape(ROWS_ALL, QW)
    out_weight = (out_values.astype(jnp.float32).reshape(QW // BLK, BLK, D // BLK, BLK) * out_scales[:, None, :, None]).reshape(QW, D).astype(jnp.bfloat16)
    return jnp.dot(heads_out, out_weight, preferred_element_type=jnp.float32).astype(jnp.bfloat16)
```

```python
import jax
import jax.numpy as jnp
import numpy as np
from jax import lax
from jax.experimental import pallas as pl
from jax.experimental.pallas import tpu as pltpu
from jax.sharding import PartitionSpec as P

HD = 192
BLK = 128
LANES = 128
PAIR = 2 * HD
HALF = HD // 2
NBLK = 42
COLS = 336
GROUPS = 16
CHIPS = 8
CTX = 2048
STEP = 1024
NEG = -1e30
F32 = jnp.float32
BF16 = jnp.bfloat16

VMEM = pl.BlockSpec(memory_space=pltpu.VMEM)
SMEM = pl.BlockSpec(memory_space=pltpu.SMEM)
ANY = pl.BlockSpec(memory_space=pl.ANY)


def iota(shape, dim):
    return lax.broadcasted_iota(jnp.int32, shape, dim)


def copies(rows):
    spread = jnp.broadcast_to(rows.reshape(GROUPS, 1, 8, LANES), (GROUPS, 4, 8, LANES))
    return spread.reshape(GROUPS * 32, LANES).astype(BF16)


def project(order, x, values, scales, keep, send, wide, blocks):
    group, core = lax.axis_index("group"), lax.axis_index("mp") % 2
    first = (21 * group) // 8
    shift = (21 * group - 8 * first) * 16
    scale = scales[...]
    rows = scale.shape[0]
    which = iota((rows, NBLK), 1)
    place = (iota((rows, COLS), 1) + shift) // BLK
    spread = jnp.zeros((rows, COLS), F32)
    for i in range(4):
        block = order[jnp.minimum(first + i, NBLK - 1)]
        column = jnp.sum(jnp.where(which == block, scale, 0.0), axis=1, keepdims=True)
        spread = jnp.where(place == i, column, spread)
    total = jnp.zeros((2 * GROUPS, COLS), F32)
    for i in range(rows):
        part = slice(i * BLK, (i + 1) * BLK)
        total += jnp.dot(x[:, part], values[part, :], preferred_element_type=F32) * spread[i : i + 1, :]
    wide[...] = jnp.zeros_like(wide)
    for i in range(3):
        end = min(COLS, (i + 1) * LANES)
        wide[:, i * LANES : end] = total[:, i * LANES : end]
    turned = pltpu.roll(wide[...], shift, 1)
    for i in range(4):
        part = slice(i * LANES, (i + 1) * LANES)
        blocks[i] = turned[:, part]
        keep[:, part] = blocks[i, pl.ds(core, GROUPS, stride=2), :]
        send[:, part] = blocks[i, pl.ds(1 - core, GROUPS, stride=2), :]


def pair_sum(keep, other, out, rows):
    for i in range(4):
        part = slice(i * LANES, (i + 1) * LANES)
        total = keep[:, part] + other[:, part]
        rows[pl.ds(i, GROUPS, stride=8), :] = total
        rows[pl.ds(i + 4, GROUPS, stride=8), :] = total
    out[...] = copies(rows[...])


def attend(order, length, freq, parts, cache, other, out, kv, sems, stored, logical, halves, rows):
    device = lax.axis_index("mp")
    core, chip = device % 2, device // 2
    steps = CTX // STEP
    transfers = []
    for half in range(2):
        source, owner = ((cache, device), (other, device + 1 - 2 * core))[half]
        for i in range(steps):
            n = half * steps + i
            copy = pltpu.make_async_copy(
                source.at[core, pl.ds(i * STEP, STEP), :], kv.at[n], sems.at[n]
            )
            copy.start()
            transfers.append((copy, owner * CTX + i * STEP))

    shape = (48, GROUPS * 32)
    col = iota(shape, 1)
    pick = ((21 * (col >> 5)) >> 3) + (col & 3) == iota(shape, 0)
    stored[...] = jnp.dot(pick.astype(F32).astype(BF16), parts[...], preferred_element_type=F32)
    logical[40:48, :] = jnp.zeros((8, LANES), F32)
    for s in range(NBLK):
        logical[pl.ds(order[s], 1), :] = stored[s : s + 1, :]
    pairs = jnp.concatenate([logical[pl.ds(t, 16, stride=3), :] for t in range(3)], axis=1)

    shape = (16, PAIR)
    row, lane = iota(shape, 0), iota(shape, 1)
    position = length[core]
    angle = position.astype(F32) * freq[...]
    cosine, sine = jnp.cos(angle), jnp.sin(angle)
    partner = jnp.where(lane % HD < HALF, -pltpu.roll(pairs, PAIR - HALF, 1), pltpu.roll(pairs, HALF, 1))
    turned = jnp.where(row == 13, pairs, pairs * cosine + partner * sine)
    turned = turned.astype(BF16).astype(F32)
    mine = (row < 6) == (lane < HD)
    used = mine & (row < 12)
    query = jnp.concatenate(
        [jnp.where(used, turned, 0.0), jnp.where(used, pltpu.roll(turned, HD, 1), 0.0)], axis=0
    )
    factor = HD ** (-0.5)
    new = jnp.sum(query * turned[12:13, :], axis=1, keepdims=True) * factor
    new = jnp.where(chip == 0, new, NEG)
    query = query.astype(BF16)

    top = new
    scores = []
    for n, (copy, base) in enumerate(transfers):
        copy.wait()
        score = lax.dot_general(
            query, kv[n, :, :PAIR], (((1,), (1,)), ((), ())), preferred_element_type=F32
        )
        valid = iota(score.shape, 1) < position - base
        score = jnp.where(valid, score * factor, NEG)
        top = jnp.maximum(top, jnp.max(score, axis=1, keepdims=True))
        scores.append((score, valid))
    own = jnp.where(chip == 0, jnp.exp(new - top), 0.0)
    total = own
    value = own * turned[13:14, :]
    for n, (score, valid) in enumerate(scores):
        weight = jnp.where(valid, jnp.exp(score - top), 0.0)
        total += jnp.sum(weight, axis=1, keepdims=True)
        value += jnp.dot(weight.astype(BF16), kv[n, :, PAIR:], preferred_element_type=F32)
    some = total > 0.0
    safe = jnp.where(some, total, 1.0)
    value = value / safe
    level = jnp.where(some, top + jnp.log(safe), NEG)

    merged = jnp.where(mine, value[:16], pltpu.roll(value[16:], HD, 1))
    low = iota((16, 1), 0) < 6
    even = jnp.where(low, level[:16], level[16:])
    odd = jnp.where(low, level[16:], level[:16])
    lane = iota((16, LANES), 1)
    for w in range(4):
        data = merged if w == 0 else pltpu.roll(merged, PAIR - HALF * w, 1)
        level = even if w < 2 else odd
        high = level.astype(BF16).astype(F32)
        middle = (level - high).astype(BF16).astype(F32)
        tail = level - high - middle
        terms = jnp.where(lane == HALF, high, jnp.where(lane == HALF + 1, middle, jnp.where(lane == HALF + 2, tail, 0.0)))
        halves[pl.ds(w, 16, stride=4), :] = jnp.where(lane < HALF, data[:, :LANES], terms)
    rows[...] = jnp.zeros_like(rows)
    for u in range(3):
        data = halves[pl.ds(u, GROUPS, stride=3), :]
        rows[pl.ds(u, GROUPS, stride=8), :] = data
        rows[pl.ds(u + 4, GROUPS, stride=8), :] = data
    out[...] = copies(rows[...])


def merge(parts, out, rows):
    shape = (LANES, LANES)
    term = iota(shape, 0)
    pick = ((term >= HALF) & (term < HALF + 3)).astype(F32).astype(BF16)
    data = parts[...]
    shape = (GROUPS, 4, 8, LANES)
    level = jnp.dot(data, pick, preferred_element_type=F32).reshape(shape)
    data = data.astype(F32).reshape(shape)

    def both(fn, x):
        x = x.reshape(GROUPS * 8, LANES)
        rows[...] = x
        turned = jnp.concatenate([rows[4:, :], rows[:4, :]], axis=0)
        sub = iota(x.shape, 0) % 8
        back = jnp.concatenate([rows[-4:, :], rows[:-4, :]], axis=0)
        return fn(x, jnp.where(sub < 4, turned, back))

    top = both(jnp.maximum, jnp.max(level, axis=1)).reshape(GROUPS, 1, 8, LANES)
    weight = jnp.exp(level - top)
    total = both(jnp.add, jnp.sum(weight, axis=1))
    value = both(jnp.add, jnp.sum(weight * data, axis=1))
    value = jnp.where(iota(value.shape, 1) < HALF, value / total, 0.0)
    rows[...] = value
    for u in range(3):
        out[u] = rows[pl.ds(u, GROUPS, stride=8), :].astype(BF16)


def project_out(mine, other, values, scales, out):
    group = lax.axis_index("group")
    first = (9 * group) // 4
    shift = (9 * group - 4 * first) * 32
    lane = iota((2 * GROUPS, LANES), 1)
    width = values.shape[1]
    total = jnp.zeros((3 * 2 * GROUPS, width), F32)
    for u in range(3):
        data = jnp.concatenate([mine[u], other[u]], axis=0)
        block = (lane + shift + HALF * u) // BLK
        data = jnp.concatenate([jnp.where(block == i, data, jnp.zeros_like(data)) for i in range(3)], axis=0)
        total += jnp.dot(
            data[:, :HALF], values[HALF * u : HALF * (u + 1), :], preferred_element_type=F32
        )
    result = jnp.zeros((2 * GROUPS, width), F32)
    cols = width // BLK
    scale = scales[...]
    for i in range(3):
        row = jnp.sum(jnp.where(iota(scale.shape, 0) == first + i, scale, 0.0), axis=0, keepdims=True)
        wide = jnp.concatenate([jnp.broadcast_to(row[:, j : j + 1], (1, BLK)) for j in range(cols)], axis=1)
        result += total[2 * GROUPS * i : 2 * GROUPS * (i + 1)] * wide
    out[:, 0, :] = result[:GROUPS]
    out[:, 1, :] = result[GROUPS:]


def finish(parts, out):
    total = jnp.sum(parts[...], axis=0)
    swapped = jnp.concatenate([total[1:2], total[0:1]], axis=0)
    out[...] = jnp.where(lax.axis_index("mp") % 2 == 0, total, swapped).astype(BF16)


def call(kernel, shapes, in_specs, scratch, args):
    single = not isinstance(shapes, (list, tuple))
    return pl.pallas_call(
        kernel,
        out_shape=shapes,
        in_specs=in_specs,
        out_specs=VMEM if single else [VMEM] * len(shapes),
        scratch_shapes=scratch,
        compiler_params=pltpu.CompilerParams(vmem_limit_bytes=40 * 1024 * 1024),
    )(*args)


def local(
    activations, qkv_values, qkv_scales, block_order, out_values, out_scales, kv_cache, cache_len
):
    both = ("group", "mp")
    width = activations.shape[1]
    swap = [(i, i ^ 1) for i in range(2 * CHIPS)]
    same_core = [
        [g * 2 * CHIPS + 2 * k + core for g in range(GROUPS) for k in range(CHIPS)] for core in range(2)
    ]

    def exchange(rows):
        chunks = rows.reshape(GROUPS * CHIPS, 4, LANES)
        chunks = lax.all_to_all(chunks, both, 0, 0, tiled=True, axis_index_groups=same_core)
        return chunks.reshape(GROUPS * 32, LANES)

    cache_other = lax.ppermute(kv_cache, "mp", swap)
    x = jnp.broadcast_to(activations[None], (GROUPS,) + activations.shape)
    x = lax.all_to_all(x, "group", 0, 0, tiled=True).reshape(2 * GROUPS, width)
    keep, send = call(
        project,
        [jax.ShapeDtypeStruct((GROUPS, 4 * LANES), F32)] * 2,
        [SMEM, VMEM, VMEM, VMEM],
        [pltpu.VMEM((2 * GROUPS, 4 * LANES), F32), pltpu.VMEM((4, 2 * GROUPS, LANES), F32)],
        (block_order, x, qkv_values, qkv_scales),
    )
    rows_type = jax.ShapeDtypeStruct((GROUPS * 32, LANES), BF16)
    rows_scratch = pltpu.VMEM((GROUPS * 8, LANES), F32)
    parts = call(
        pair_sum, rows_type, [VMEM, VMEM], [rows_scratch], (keep, lax.ppermute(send, "mp", swap))
    )
    parts = exchange(parts)
    lanes = np.arange(PAIR) % HALF
    freq = (10000.0 ** (-lanes / HALF)).astype(np.float32)[None, :]
    steps = 2 * CTX // STEP
    parts = call(
        attend,
        rows_type,
        [SMEM, SMEM, VMEM, VMEM, ANY, ANY],
        [
            pltpu.VMEM((steps, STEP, 2 * PAIR), BF16),
            pltpu.SemaphoreType.DMA((steps,)),
            pltpu.VMEM((48, LANES), F32),
            pltpu.VMEM((48, LANES), F32),
            pltpu.VMEM((64, LANES), F32),
            rows_scratch,
        ],
        (block_order, cache_len, jnp.asarray(freq), parts, kv_cache, cache_other),
    )
    parts = exchange(parts)
    heads = call(
        merge, jax.ShapeDtypeStruct((3, GROUPS, LANES), BF16), [VMEM], [rows_scratch], (parts,)
    )
    result = call(
        project_out,
        jax.ShapeDtypeStruct((GROUPS, 2, width), F32),
        [VMEM] * 4,
        [],
        (heads, lax.ppermute(heads, "mp", swap), out_values, out_scales),
    )
    result = lax.all_to_all(result, "group", 0, 0, tiled=True)
    return call(finish, jax.ShapeDtypeStruct((2, width), BF16), [VMEM], [], (result,))


def solution(mesh):
    placed = (
        P("group", "mp"),
        P("mp", "group"),
        P("mp", None),
        P(),
        P("group", "mp"),
        P(None, "mp"),
        P("group", "mp", None),
        P("group"),
    )
    return jax.shard_map(
        local, mesh=mesh, in_specs=placed, out_specs=P("group", "mp"), check_vma=False
    )
```

```python
import jax
import jax.numpy as jnp
import numpy as np
from jax import lax
from jax.experimental import pallas as pl
from jax.experimental.pallas import tpu as pltpu
from jax.sharding import PartitionSpec as P

HD = 192
BLK = 128
LANES = 128
PAIR = 2 * HD
HALF = HD // 2
NBLK = 42
COLS = 336
GROUPS = 16
CHIPS = 8
CTX = 2048
STEP = 2048
NEG = -1e30
F32 = jnp.float32
BF16 = jnp.bfloat16

VMEM = pl.BlockSpec(memory_space=pltpu.VMEM)
SMEM = pl.BlockSpec(memory_space=pltpu.SMEM)
HBM = pl.BlockSpec(memory_space=pltpu.HBM)


def iota(shape, dim):
    return lax.broadcasted_iota(jnp.int32, shape, dim)


def copies(rows):
    spread = jnp.broadcast_to(rows.reshape(GROUPS, 1, 8, LANES), (GROUPS, 4, 8, LANES))
    return spread.reshape(GROUPS * 32, LANES).astype(BF16)


def prepare(
    order_in, length_in, freq_in, values, scales_in, cache,
    weight, spread, pick, table, mine,
    order, length, freq, scales, sems,
):
    group, core = lax.axis_index("group"), lax.axis_index("mp") % 2
    pairs = (
        (order_in, order),
        (length_in, length),
        (scales_in, scales),
        (freq_in, freq),
        (values, weight),
        (cache.at[core, :, pl.ds(0, PAIR)], mine),
    )
    transfers = [
        pltpu.make_async_copy(source, target, sems.at[i]) for i, (source, target) in enumerate(pairs)
    ]
    for transfer in transfers:
        transfer.start()
    for transfer in transfers[:4]:
        transfer.wait()
    first = (21 * group) // 8
    shift = (21 * group - 8 * first) * 16
    scale = scales[...]
    rows = scale.shape[0]
    which = iota((rows, NBLK), 1)
    place = (iota((rows, COLS), 1) + shift) // BLK
    columns = jnp.zeros((rows, COLS), F32)
    for i in range(4):
        block = order[jnp.minimum(first + i, NBLK - 1)]
        column = jnp.sum(jnp.where(which == block, scale, 0.0), axis=1, keepdims=True)
        columns = jnp.where(place == i, column, columns)
    spread[...] = columns
    shape = (48, GROUPS * 32)
    col = iota(shape, 1)
    stored = ((21 * (col >> 5)) >> 3) + (col & 3) == iota(shape, 0)
    shape = (48, 48)
    row, col = iota(shape, 0), iota(shape, 1)
    moved = jnp.zeros(shape, F32)
    for s in range(NBLK):
        moved = jnp.where((col == s) & (row == order[s]), 1.0, moved)
    pick[...] = jnp.dot(
        moved.astype(BF16), stored.astype(F32).astype(BF16), preferred_element_type=F32
    ).astype(BF16)
    position = length[core].astype(F32)
    angle = position * freq[...]
    table[0:1, :] = jnp.cos(angle)
    table[1:2, :] = jnp.sin(angle)
    table[2:8, :] = jnp.full((6, PAIR), position, F32)
    for transfer in transfers[4:]:
        transfer.wait()


def project(x, weight, spread, keep, send, wide, blocks):
    group, core = lax.axis_index("group"), lax.axis_index("mp") % 2
    shift = (21 * group) % 8 * 16
    total = jnp.zeros((2 * GROUPS, COLS), F32)
    for i in range(spread.shape[0]):
        part = slice(i * BLK, (i + 1) * BLK)
        dot = lax.dot_general(
            x[:, part], weight[:, part], (((1,), (1,)), ((), ())), preferred_element_type=F32
        )
        total += dot * spread[i : i + 1, :]
    wide[...] = jnp.zeros_like(wide)
    for i in range(3):
        end = min(COLS, (i + 1) * LANES)
        wide[:, i * LANES : end] = total[:, i * LANES : end]
    turned = pltpu.roll(wide[...], shift, 1)
    for i in range(4):
        part = slice(i * LANES, (i + 1) * LANES)
        blocks[i] = turned[:, part]
        keep[:, part] = blocks[i, pl.ds(core, GROUPS, stride=2), :]
        send[:, part] = blocks[i, pl.ds(1 - core, GROUPS, stride=2), :]


def pair_sum(keep, other, out, rows):
    for i in range(4):
        part = slice(i * LANES, (i + 1) * LANES)
        total = keep[:, part] + other[:, part]
        rows[pl.ds(i, GROUPS, stride=8), :] = total
        rows[pl.ds(i + 4, GROUPS, stride=8), :] = total
    out[...] = copies(rows[...])


def attend(table, pick, parts, mine, cache, other, out, keys, values, sems, logical, halves, rows):
    device = lax.axis_index("mp")
    core, chip = device % 2, device // 2
    steps = CTX // STEP
    transfers = []
    for source, lane, target in ((other, 0, keys), (cache, PAIR, values.at[0]), (other, PAIR, values.at[1])):
        for i in range(steps):
            part = pl.ds(i * STEP, STEP)
            copy = pltpu.make_async_copy(
                source.at[core, part, pl.ds(lane, PAIR)], target.at[part, :], sems.at[len(transfers)]
            )
            copy.start()
            transfers.append(copy)

    logical[...] = jnp.dot(pick[...], parts[...], preferred_element_type=F32)
    pairs = jnp.concatenate([logical[pl.ds(t, 16, stride=3), :] for t in range(3)], axis=1)

    shape = (16, PAIR)
    row, lane = iota(shape, 0), iota(shape, 1)
    cosine, sine = table[0:1, :], table[1:2, :]
    position = table[2:3, :1].astype(jnp.int32)
    partner = jnp.where(lane % HD < HALF, -pltpu.roll(pairs, PAIR - HALF, 1), pltpu.roll(pairs, HALF, 1))
    turned = jnp.where(row == 13, pairs, pairs * cosine + partner * sine)
    turned = turned.astype(BF16).astype(F32)
    own_head = (row < 6) == (lane < HD)
    used = own_head & (row < 12)
    query = jnp.concatenate(
        [jnp.where(used, turned, 0.0), jnp.where(used, pltpu.roll(turned, HD, 1), 0.0)], axis=0
    )
    factor = HD ** (-0.5)
    new = jnp.sum(query * turned[12:13, :], axis=1, keepdims=True) * factor
    new = jnp.where(chip == 0, new, NEG)
    query = query.astype(BF16)

    top = new
    scores = []
    for n in range(2 * steps):
        half, i = divmod(n, steps)
        if half:
            transfers[i].wait()
        part = slice(i * STEP, (i + 1) * STEP)
        base = (device, device + 1 - 2 * core)[half] * CTX + i * STEP
        score = lax.dot_general(
            query, (mine, keys)[half][part, :], (((1,), (1,)), ((), ())), preferred_element_type=F32
        )
        valid = iota(score.shape, 1) < position - base
        score = jnp.where(valid, score * factor, NEG)
        top = jnp.maximum(top, jnp.max(score, axis=1, keepdims=True))
        scores.append((score, valid))
    own = jnp.where(chip == 0, jnp.exp(new - top), 0.0)
    total = own
    value = own * turned[13:14, :]
    for n, (score, valid) in enumerate(scores):
        half, i = divmod(n, steps)
        transfers[steps + n].wait()
        weight = jnp.where(valid, jnp.exp(score - top), 0.0)
        total += jnp.sum(weight, axis=1, keepdims=True)
        value += jnp.dot(weight.astype(BF16), values[half, i * STEP : (i + 1) * STEP, :], preferred_element_type=F32)
    some = total > 0.0
    safe = jnp.where(some, total, 1.0)
    value = value / safe
    level = jnp.where(some, top + jnp.log(safe), NEG)

    merged = jnp.where(own_head, value[:16], pltpu.roll(value[16:], HD, 1))
    low = iota((16, 1), 0) < 6
    even = jnp.where(low, level[:16], level[16:])
    odd = jnp.where(low, level[16:], level[:16])
    lane = iota((16, LANES), 1)
    for w in range(4):
        data = merged if w == 0 else pltpu.roll(merged, PAIR - HALF * w, 1)
        level = even if w < 2 else odd
        high = level.astype(BF16).astype(F32)
        middle = (level - high).astype(BF16).astype(F32)
        tail = level - high - middle
        terms = jnp.where(lane == HALF, high, jnp.where(lane == HALF + 1, middle, jnp.where(lane == HALF + 2, tail, 0.0)))
        halves[pl.ds(w, 16, stride=4), :] = jnp.where(lane < HALF, data[:, :LANES], terms)
    rows[...] = jnp.zeros_like(rows)
    for u in range(3):
        data = halves[pl.ds(u, GROUPS, stride=3), :]
        rows[pl.ds(u, GROUPS, stride=8), :] = data
        rows[pl.ds(u + 4, GROUPS, stride=8), :] = data
    out[...] = copies(rows[...])


def merge(parts, out, rows):
    shape = (LANES, LANES)
    term = iota(shape, 0)
    pick = ((term >= HALF) & (term < HALF + 3)).astype(F32).astype(BF16)
    data = parts[...]
    shape = (GROUPS, 4, 8, LANES)
    level = jnp.dot(data, pick, preferred_element_type=F32).reshape(shape)
    data = data.astype(F32).reshape(shape)

    def both(fn, x):
        x = x.reshape(GROUPS * 8, LANES)
        rows[...] = x
        turned = jnp.concatenate([rows[4:, :], rows[:4, :]], axis=0)
        sub = iota(x.shape, 0) % 8
        back = jnp.concatenate([rows[-4:, :], rows[:-4, :]], axis=0)
        return fn(x, jnp.where(sub < 4, turned, back))

    top = both(jnp.maximum, jnp.max(level, axis=1)).reshape(GROUPS, 1, 8, LANES)
    weight = jnp.exp(level - top)
    total = both(jnp.add, jnp.sum(weight, axis=1))
    value = both(jnp.add, jnp.sum(weight * data, axis=1))
    value = jnp.where(iota(value.shape, 1) < HALF, value / total, 0.0)
    rows[...] = value
    for u in range(3):
        out[u] = rows[pl.ds(u, GROUPS, stride=8), :].astype(BF16)


def project_out(mine, other, values, scales, out, rows):
    first = (9 * lax.axis_index("group")) // 4
    group = lax.axis_index("group")
    shift = (9 * group) % 4 * 32
    lane = iota((2 * GROUPS, LANES), 1)
    width = values.shape[1]
    total = jnp.zeros((3 * 2 * GROUPS, width), F32)
    for u in range(3):
        data = jnp.concatenate([mine[u], other[u]], axis=0)
        block = (lane + shift + HALF * u) // BLK
        data = jnp.concatenate([jnp.where(block == i, data, jnp.zeros_like(data)) for i in range(3)], axis=0)
        total += jnp.dot(
            data[:, :HALF], values[HALF * u : HALF * (u + 1), :], preferred_element_type=F32
        )
    result = jnp.zeros((2 * GROUPS, width), F32)
    scale = scales[...]
    for i in range(3):
        column = jnp.sum(jnp.where(iota(scale.shape, 1) == first + i, scale, 0.0), axis=1, keepdims=True)
        wide = [jnp.broadcast_to(column[j : j + 1, :], (1, BLK)) for j in range(scale.shape[0])]
        result += total[2 * GROUPS * i : 2 * GROUPS * (i + 1)] * jnp.concatenate(wide, axis=1)
    rows[:, 0, :] = result[:GROUPS]
    rows[:, 1, :] = result[GROUPS:]
    out[...] = rows[...].astype(BF16)


def finish(parts, out):
    total = jnp.sum(parts[...].astype(F32), axis=0)
    swapped = jnp.concatenate([total[1:2], total[0:1]], axis=0)
    out[...] = jnp.where(lax.axis_index("mp") % 2 == 0, total, swapped).astype(BF16)


def call(kernel, shapes, in_specs, scratch, args, limit=16):
    single = not isinstance(shapes, (list, tuple))
    args = [
        pltpu.with_memory_space_constraint(arg, pltpu.HBM) if spec is HBM else arg
        for arg, spec in zip(args, in_specs)
    ]
    return pl.pallas_call(
        kernel,
        out_shape=shapes,
        in_specs=in_specs,
        out_specs=VMEM if single else [VMEM] * len(shapes),
        scratch_shapes=scratch,
        compiler_params=pltpu.CompilerParams(vmem_limit_bytes=limit * 1024 * 1024),
    )(*args)


def local(
    activations, qkv_values, qkv_scales, block_order, out_values, out_scales, kv_cache, cache_len
):
    both = ("group", "mp")
    width = activations.shape[1]
    swap = [(i, i ^ 1) for i in range(2 * CHIPS)]
    same_core = [
        [g * 2 * CHIPS + 2 * k + core for g in range(GROUPS) for k in range(CHIPS)] for core in range(2)
    ]

    def exchange(rows):
        chunks = rows.reshape(GROUPS * CHIPS, 4, LANES)
        chunks = lax.all_to_all(chunks, both, 0, 0, tiled=True, axis_index_groups=same_core)
        return chunks.reshape(GROUPS * 32, LANES)

    cache_other = lax.ppermute(kv_cache, "mp", swap)
    x = jnp.broadcast_to(activations[None], (GROUPS,) + activations.shape)
    x = lax.all_to_all(x, "group", 0, 0, tiled=True).reshape(2 * GROUPS, width)
    lanes = np.arange(PAIR) % HALF
    freq = (10000.0 ** (-lanes / HALF)).astype(np.float32)[None, :]
    weight, spread, pick, table, keys_mine = call(
        prepare,
        [
            jax.ShapeDtypeStruct((COLS, width), BF16),
            jax.ShapeDtypeStruct((width // BLK, COLS), F32),
            jax.ShapeDtypeStruct((48, GROUPS * 32), BF16),
            jax.ShapeDtypeStruct((8, PAIR), F32),
            jax.ShapeDtypeStruct((CTX, PAIR), BF16),
        ],
        [HBM] * 6,
        [
            pltpu.SMEM(block_order.shape, jnp.int32),
            pltpu.SMEM(cache_len.shape, jnp.int32),
            pltpu.VMEM(freq.shape, F32),
            pltpu.VMEM(qkv_scales.shape, F32),
            pltpu.SemaphoreType.DMA((6,)),
        ],
        (block_order, cache_len, jnp.asarray(freq), qkv_values.T, qkv_scales, kv_cache),
    )
    keep, send = call(
        project,
        [jax.ShapeDtypeStruct((GROUPS, 4 * LANES), F32)] * 2,
        [VMEM, VMEM, VMEM],
        [pltpu.VMEM((2 * GROUPS, 4 * LANES), F32), pltpu.VMEM((4, 2 * GROUPS, LANES), F32)],
        (x, weight, spread),
    )
    rows_type = jax.ShapeDtypeStruct((GROUPS * 32, LANES), BF16)
    rows_scratch = pltpu.VMEM((GROUPS * 8, LANES), F32)
    parts = call(
        pair_sum, rows_type, [VMEM, VMEM], [rows_scratch], (keep, lax.ppermute(send, "mp", swap))
    )
    parts = exchange(parts)
    parts = call(
        attend,
        rows_type,
        [VMEM, VMEM, VMEM, VMEM, HBM, HBM],
        [
            pltpu.VMEM((CTX, PAIR), BF16),
            pltpu.VMEM((2, CTX, PAIR), BF16),
            pltpu.SemaphoreType.DMA((3 * CTX // STEP,)),
            pltpu.VMEM((48, LANES), F32),
            pltpu.VMEM((64, LANES), F32),
            rows_scratch,
        ],
        (table, pick, parts, keys_mine, kv_cache, cache_other),
    )
    parts = exchange(parts)
    heads = call(
        merge, jax.ShapeDtypeStruct((3, GROUPS, LANES), BF16), [VMEM], [rows_scratch], (parts,)
    )
    result = call(
        project_out,
        jax.ShapeDtypeStruct((GROUPS, 2, width), BF16),
        [VMEM] * 4,
        [pltpu.VMEM((GROUPS, 2, width), F32)],
        (heads, lax.ppermute(heads, "mp", swap), out_values, out_scales.T),
    )
    result = lax.all_to_all(result, "group", 0, 0, tiled=True)
    return call(finish, jax.ShapeDtypeStruct((2, width), BF16), [VMEM], [], (result,))


def solution(mesh):
    placed = (
        P("group", "mp"),
        P("mp", "group"),
        P("mp", None),
        P(),
        P("group", "mp"),
        P(None, "mp"),
        P("group", "mp", None),
        P("group"),
    )
    return jax.shard_map(
        local, mesh=mesh, in_specs=placed, out_specs=P("group", "mp"), check_vma=False
    )
```

```python
import jax
import jax.numpy as jnp
import numpy as np
from jax import lax
from jax.experimental import pallas as pl
from jax.experimental.pallas import tpu as pltpu
from jax.sharding import PartitionSpec as P

HD = 192
BLK = 128
LANES = 128
PAIR = 2 * HD
HALF = HD // 2
NBLK = 42
COLS = 336
GROUPS = 16
CHIPS = 8
FAR = 10
FAR_CHIP = 4
CTX = 2048
EARLY = 1024
NEG = -1e30
F32 = jnp.float32
BF16 = jnp.bfloat16

VMEM = pl.BlockSpec(memory_space=pltpu.VMEM)
SMEM = pl.BlockSpec(memory_space=pltpu.SMEM)
HBM = pl.BlockSpec(memory_space=pltpu.HBM)


def iota(shape, dim):
    return lax.broadcasted_iota(jnp.int32, shape, dim)


def copies(rows):
    spread = jnp.broadcast_to(rows.reshape(GROUPS, 1, 8, LANES), (GROUPS, 4, 8, LANES))
    return spread.reshape(GROUPS * 32, LANES).astype(BF16)


def prepare(
    order_in, length_in, freq_in, values, scales_in, cache,
    weight, spread, pick, table, mine,
    order, length, freq, scales, sems,
):
    group, core = lax.axis_index("group"), lax.axis_index("mp") % 2
    pairs = (
        (order_in, order),
        (length_in, length),
        (scales_in, scales),
        (freq_in, freq),
        (values, weight),
        (cache.at[core, :, pl.ds(0, PAIR)], mine.at[pl.ds(0, CTX), :]),
        (cache.at[core, pl.ds(0, EARLY), pl.ds(PAIR, PAIR)], mine.at[pl.ds(CTX, EARLY), :]),
    )
    transfers = [
        pltpu.make_async_copy(source, target, sems.at[i]) for i, (source, target) in enumerate(pairs)
    ]
    for transfer in transfers:
        transfer.start()
    for transfer in transfers[:4]:
        transfer.wait()
    first = (21 * group) // 8
    shift = (21 * group - 8 * first) * 16
    scale = scales[...]
    rows = scale.shape[0]
    which = iota((rows, NBLK), 1)
    place = (iota((rows, COLS), 1) + shift) // BLK
    columns = jnp.zeros((rows, COLS), F32)
    for i in range(4):
        block = order[jnp.minimum(first + i, NBLK - 1)]
        column = jnp.sum(jnp.where(which == block, scale, 0.0), axis=1, keepdims=True)
        columns = jnp.where(place == i, column, columns)
    spread[...] = columns
    shape = (48, GROUPS * 32)
    col = iota(shape, 1)
    stored = ((21 * ((col >> 5) ^ FAR)) >> 3) + (col & 3) == iota(shape, 0)
    shape = (48, 48)
    row, col = iota(shape, 0), iota(shape, 1)
    moved = jnp.zeros(shape, F32)
    for s in range(NBLK):
        moved = jnp.where((col == s) & (row == order[s]), 1.0, moved)
    pick[...] = jnp.dot(
        moved.astype(BF16), stored.astype(F32).astype(BF16), preferred_element_type=F32
    ).astype(BF16)
    position = length[core].astype(F32)
    angle = position * freq[...]
    table[0:1, :] = jnp.cos(angle)
    table[1:2, :] = jnp.sin(angle)
    table[2:8, :] = jnp.full((6, PAIR), position, F32)
    for transfer in transfers[4:]:
        transfer.wait()


def project(x, weight, spread, keep, send, wide, blocks):
    group, core = lax.axis_index("group"), lax.axis_index("mp") % 2
    shift = (21 * group) % 8 * 16
    total = jnp.zeros((2 * GROUPS, COLS), F32)
    for i in range(spread.shape[0]):
        part = slice(i * BLK, (i + 1) * BLK)
        dot = lax.dot_general(
            x[:, part], weight[:, part], (((1,), (1,)), ((), ())), preferred_element_type=F32
        )
        total += dot * spread[i : i + 1, :]
    wide[...] = jnp.zeros_like(wide)
    for i in range(3):
        end = min(COLS, (i + 1) * LANES)
        wide[:, i * LANES : end] = total[:, i * LANES : end]
    turned = pltpu.roll(wide[...], shift, 1)
    for i in range(4):
        part = slice(i * LANES, (i + 1) * LANES)
        blocks[i] = turned[:, part]
        keep[:, part] = blocks[i, pl.ds(core, GROUPS, stride=2), :]
        send[:, part] = blocks[i, pl.ds(1 - core, GROUPS, stride=2), :]


def pair_sum(keep, other, out, rows):
    for i in range(4):
        part = slice(i * LANES, (i + 1) * LANES)
        total = keep[:, part] + other[:, part]
        rows[pl.ds(i, GROUPS, stride=8), :] = total
        rows[pl.ds(i + 4, GROUPS, stride=8), :] = total
    out[...] = copies(rows[...])


def attend(table, pick, parts, mine, cache, other, out, keys, values, sems, logical, halves, rows):
    device = lax.axis_index("mp")
    core, chip = device % 2, device // 2
    transfers = []
    moves = (
        (other.at[core, :, pl.ds(0, PAIR)], keys),
        (cache.at[core, pl.ds(EARLY, CTX - EARLY), pl.ds(PAIR, PAIR)], values.at[pl.ds(0, CTX - EARLY), :]),
        (other.at[core, :, pl.ds(PAIR, PAIR)], values.at[pl.ds(CTX - EARLY, CTX), :]),
    )
    for i, (source, target) in enumerate(moves):
        copy = pltpu.make_async_copy(source, target, sems.at[i])
        copy.start()
        transfers.append(copy)

    logical[...] = jnp.dot(pick[...], parts[...], preferred_element_type=F32)
    pairs = jnp.concatenate([logical[pl.ds(t, 16, stride=3), :] for t in range(3)], axis=1)

    shape = (16, PAIR)
    row, lane = iota(shape, 0), iota(shape, 1)
    cosine, sine = table[0:1, :], table[1:2, :]
    position = table[2:3, :1].astype(jnp.int32)
    partner = jnp.where(lane % HD < HALF, -pltpu.roll(pairs, PAIR - HALF, 1), pltpu.roll(pairs, HALF, 1))
    turned = jnp.where(row == 13, pairs, pairs * cosine + partner * sine)
    turned = turned.astype(BF16).astype(F32)
    own_head = (row < 6) == (lane < HD)
    used = own_head & (row < 12)
    query = jnp.concatenate(
        [jnp.where(used, turned, 0.0), jnp.where(used, pltpu.roll(turned, HD, 1), 0.0)], axis=0
    )
    factor = HD ** (-0.5)
    new = jnp.sum(query * turned[12:13, :], axis=1, keepdims=True) * factor
    new = jnp.where(chip == 0, new, NEG)
    query = query.astype(BF16)

    top = new
    scores = []
    for half, source in enumerate((mine, keys)):
        if half:
            transfers[0].wait()
        base = (device, device + 1 - 2 * core)[half] * CTX
        score = lax.dot_general(
            query, source[:CTX, :], (((1,), (1,)), ((), ())), preferred_element_type=F32
        )
        valid = iota(score.shape, 1) < position - base
        score = jnp.where(valid, score * factor, NEG)
        top = jnp.maximum(top, jnp.max(score, axis=1, keepdims=True))
        scores.append((score, valid))
    own = jnp.where(chip == 0, jnp.exp(new - top), 0.0)
    total = own
    value = own * turned[13:14, :]
    weights = []
    for score, valid in scores:
        weight = jnp.where(valid, jnp.exp(score - top), 0.0)
        total += jnp.sum(weight, axis=1, keepdims=True)
        weights.append(weight.astype(BF16))
    value += jnp.dot(weights[0][:, :EARLY], mine[CTX:, :], preferred_element_type=F32)
    transfers[1].wait()
    value += jnp.dot(
        weights[0][:, EARLY:], values[: CTX - EARLY, :], preferred_element_type=F32
    )
    transfers[2].wait()
    value += jnp.dot(weights[1], values[CTX - EARLY :, :], preferred_element_type=F32)
    some = total > 0.0
    safe = jnp.where(some, total, 1.0)
    value = value / safe
    level = jnp.where(some, top + jnp.log(safe), NEG)

    merged = jnp.where(own_head, value[:16], pltpu.roll(value[16:], HD, 1))
    low = iota((16, 1), 0) < 6
    even = jnp.where(low, level[:16], level[16:])
    odd = jnp.where(low, level[16:], level[:16])
    lane = iota((16, LANES), 1)
    for w in range(4):
        data = merged if w == 0 else pltpu.roll(merged, PAIR - HALF * w, 1)
        level = even if w < 2 else odd
        high = level.astype(BF16).astype(F32)
        middle = (level - high).astype(BF16).astype(F32)
        tail = level - high - middle
        terms = jnp.where(lane == HALF, high, jnp.where(lane == HALF + 1, middle, jnp.where(lane == HALF + 2, tail, 0.0)))
        halves[pl.ds(w, 16, stride=4), :] = jnp.where(lane < HALF, data[:, :LANES], terms)
    rows[...] = jnp.zeros_like(rows)
    for u in range(3):
        data = halves[pl.ds(u, GROUPS, stride=3), :]
        rows[pl.ds(u, GROUPS, stride=8), :] = data
        rows[pl.ds(u + 4, GROUPS, stride=8), :] = data
    data = rows[...].reshape(GROUPS, 8, LANES)
    out[...] = copies(jnp.concatenate([data[p ^ FAR] for p in range(GROUPS)], axis=0))


def merge(parts, out, rows):
    shape = (LANES, LANES)
    term = iota(shape, 0)
    pick = ((term >= HALF) & (term < HALF + 3)).astype(F32).astype(BF16)
    data = parts[...]
    shape = (GROUPS, 4, 8, LANES)
    level = jnp.dot(data, pick, preferred_element_type=F32).reshape(shape)
    data = data.astype(F32).reshape(shape)

    def both(fn, x):
        x = x.reshape(GROUPS * 8, LANES)
        rows[...] = x
        turned = jnp.concatenate([rows[4:, :], rows[:4, :]], axis=0)
        sub = iota(x.shape, 0) % 8
        back = jnp.concatenate([rows[-4:, :], rows[:-4, :]], axis=0)
        return fn(x, jnp.where(sub < 4, turned, back))

    top = both(jnp.maximum, jnp.max(level, axis=1)).reshape(GROUPS, 1, 8, LANES)
    weight = jnp.exp(level - top)
    total = both(jnp.add, jnp.sum(weight, axis=1))
    value = both(jnp.add, jnp.sum(weight * data, axis=1))
    value = jnp.where(iota(value.shape, 1) < HALF, value / total, 0.0)
    rows[...] = value
    for u in range(3):
        out[u] = rows[pl.ds(u, GROUPS, stride=8), :].astype(BF16)


def project_out(mine, other, values, scales, out, rows):
    first = (9 * lax.axis_index("group")) // 4
    group = lax.axis_index("group")
    shift = (9 * group) % 4 * 32
    lane = iota((2 * GROUPS, LANES), 1)
    width = values.shape[1]
    total = jnp.zeros((3 * 2 * GROUPS, width), F32)
    for u in range(3):
        data = jnp.concatenate([mine[u], other[u]], axis=0)
        block = (lane + shift + HALF * u) // BLK
        data = jnp.concatenate([jnp.where(block == i, data, jnp.zeros_like(data)) for i in range(3)], axis=0)
        total += jnp.dot(
            data[:, :HALF], values[HALF * u : HALF * (u + 1), :], preferred_element_type=F32
        )
    result = jnp.zeros((2 * GROUPS, width), F32)
    scale = scales[...]
    for i in range(3):
        column = jnp.sum(jnp.where(iota(scale.shape, 1) == first + i, scale, 0.0), axis=1, keepdims=True)
        wide = [jnp.broadcast_to(column[j : j + 1, :], (1, BLK)) for j in range(scale.shape[0])]
        result += total[2 * GROUPS * i : 2 * GROUPS * (i + 1)] * jnp.concatenate(wide, axis=1)
    rows[:, 0, :] = result[:GROUPS]
    rows[:, 1, :] = result[GROUPS:]
    out[...] = rows[...].astype(BF16)


def finish(parts, out):
    total = jnp.sum(parts[...].astype(F32), axis=0)
    swapped = jnp.concatenate([total[1:2], total[0:1]], axis=0)
    out[...] = jnp.where(lax.axis_index("mp") % 2 == 0, total, swapped).astype(BF16)


def call(kernel, shapes, in_specs, scratch, args, limit=16):
    single = not isinstance(shapes, (list, tuple))
    args = [
        pltpu.with_memory_space_constraint(arg, pltpu.HBM) if spec is HBM else arg
        for arg, spec in zip(args, in_specs)
    ]
    return pl.pallas_call(
        kernel,
        out_shape=shapes,
        in_specs=in_specs,
        out_specs=VMEM if single else [VMEM] * len(shapes),
        scratch_shapes=scratch,
        compiler_params=pltpu.CompilerParams(vmem_limit_bytes=limit * 1024 * 1024),
    )(*args)


def local(
    activations, qkv_values, qkv_scales, block_order, out_values, out_scales, kv_cache, cache_len
):
    both = ("group", "mp")
    width = activations.shape[1]
    swap = [(i, i ^ 1) for i in range(2 * CHIPS)]
    same_core = [
        [(g ^ FAR) * 2 * CHIPS + 2 * (k ^ FAR_CHIP) + core for g in range(GROUPS) for k in range(CHIPS)]
        for core in range(2)
    ]
    groups = [[g ^ FAR for g in range(GROUPS)]]

    def exchange(rows):
        chunks = rows.reshape(GROUPS * CHIPS, 4, LANES)
        chunks = lax.all_to_all(chunks, both, 0, 0, tiled=True, axis_index_groups=same_core)
        return chunks.reshape(GROUPS * 32, LANES)

    cache_other = lax.ppermute(kv_cache, "mp", swap)
    x = jnp.broadcast_to(activations[None], (GROUPS,) + activations.shape)
    x = lax.all_to_all(x, "group", 0, 0, tiled=True, axis_index_groups=groups).reshape(2 * GROUPS, width)
    lanes = np.arange(PAIR) % HALF
    freq = (10000.0 ** (-lanes / HALF)).astype(np.float32)[None, :]
    weight, spread, pick, table, keys_mine = call(
        prepare,
        [
            jax.ShapeDtypeStruct((COLS, width), BF16),
            jax.ShapeDtypeStruct((width // BLK, COLS), F32),
            jax.ShapeDtypeStruct((48, GROUPS * 32), BF16),
            jax.ShapeDtypeStruct((8, PAIR), F32),
            jax.ShapeDtypeStruct((CTX + EARLY, PAIR), BF16),
        ],
        [HBM] * 6,
        [
            pltpu.SMEM(block_order.shape, jnp.int32),
            pltpu.SMEM(cache_len.shape, jnp.int32),
            pltpu.VMEM(freq.shape, F32),
            pltpu.VMEM(qkv_scales.shape, F32),
            pltpu.SemaphoreType.DMA((7,)),
        ],
        (block_order, cache_len, jnp.asarray(freq), qkv_values.T, qkv_scales, kv_cache),
    )
    keep, send = call(
        project,
        [jax.ShapeDtypeStruct((GROUPS, 4 * LANES), F32)] * 2,
        [VMEM, VMEM, VMEM],
        [pltpu.VMEM((2 * GROUPS, 4 * LANES), F32), pltpu.VMEM((4, 2 * GROUPS, LANES), F32)],
        (x, weight, spread),
    )
    rows_type = jax.ShapeDtypeStruct((GROUPS * 32, LANES), BF16)
    rows_scratch = pltpu.VMEM((GROUPS * 8, LANES), F32)
    parts = call(
        pair_sum, rows_type, [VMEM, VMEM], [rows_scratch], (keep, lax.ppermute(send, "mp", swap))
    )
    parts = exchange(parts)
    parts = call(
        attend,
        rows_type,
        [VMEM, VMEM, VMEM, VMEM, HBM, HBM],
        [
            pltpu.VMEM((CTX, PAIR), BF16),
            pltpu.VMEM((2 * CTX - EARLY, PAIR), BF16),
            pltpu.SemaphoreType.DMA((3,)),
            pltpu.VMEM((48, LANES), F32),
            pltpu.VMEM((64, LANES), F32),
            rows_scratch,
        ],
        (table, pick, parts, keys_mine, kv_cache, cache_other),
    )
    parts = exchange(parts)
    heads = call(
        merge, jax.ShapeDtypeStruct((3, GROUPS, LANES), BF16), [VMEM], [rows_scratch], (parts,)
    )
    result = call(
        project_out,
        jax.ShapeDtypeStruct((GROUPS, 2, width), BF16),
        [VMEM] * 4,
        [pltpu.VMEM((GROUPS, 2, width), F32)],
        (heads, lax.ppermute(heads, "mp", swap), out_values, out_scales.T),
    )
    result = lax.all_to_all(result, "group", 0, 0, tiled=True, axis_index_groups=groups)
    return call(finish, jax.ShapeDtypeStruct((2, width), BF16), [VMEM], [], (result,))


def solution(mesh):
    placed = (
        P("group", "mp"),
        P("mp", "group"),
        P("mp", None),
        P(),
        P("group", "mp"),
        P(None, "mp"),
        P("group", "mp", None),
        P("group"),
    )
    return jax.shard_map(
        local, mesh=mesh, in_specs=placed, out_specs=P("group", "mp"), check_vma=False
    )
```

```python
import jax
import jax.numpy as jnp
import numpy as np
from jax import lax
from jax.experimental import pallas as pl
from jax.experimental.pallas import tpu as pltpu
from jax.sharding import PartitionSpec as P

HD = 192
BLK = 128
LANES = 128
PAIR = 2 * HD
HALF = HD // 2
NBLK = 42
COLS = 336
GROUPS = 16
CHIPS = 8
FAR = 10
FAR_CHIP = 4
CTX = 2048
EARLY = 1024
NEG = -1e30
F32 = jnp.float32
BF16 = jnp.bfloat16

VMEM = pl.BlockSpec(memory_space=pltpu.VMEM)
SMEM = pl.BlockSpec(memory_space=pltpu.SMEM)
HBM = pl.BlockSpec(memory_space=pltpu.HBM)


def iota(shape, dim):
    return lax.broadcasted_iota(jnp.int32, shape, dim)


def copies(rows):
    spread = jnp.broadcast_to(rows.reshape(GROUPS, 1, 8, LANES), (GROUPS, 4, 8, LANES))
    return spread.reshape(GROUPS * 32, LANES).astype(BF16)


def prepare(
    order_in, length_in, freq_in, values, scales_in, cache,
    weight, spread, pick, table, mine,
    order, length, freq, scales, sems,
):
    group, core = lax.axis_index("group"), lax.axis_index("mp") % 2
    pairs = (
        (order_in, order),
        (length_in, length),
        (scales_in, scales),
        (freq_in, freq),
        (values, weight),
        (cache.at[core, :, pl.ds(0, PAIR)], mine.at[pl.ds(0, CTX), :]),
        (cache.at[core, pl.ds(0, EARLY), pl.ds(PAIR, PAIR)], mine.at[pl.ds(CTX, EARLY), :]),
    )
    transfers = [
        pltpu.make_async_copy(source, target, sems.at[i]) for i, (source, target) in enumerate(pairs)
    ]
    for transfer in transfers:
        transfer.start()
    for transfer in transfers[:4]:
        transfer.wait()
    first = (21 * group) // 8
    shift = (21 * group - 8 * first) * 16
    scale = scales[...]
    rows = scale.shape[0]
    which = iota((rows, NBLK), 1)
    place = (iota((rows, COLS), 1) + shift) // BLK
    columns = jnp.zeros((rows, COLS), F32)
    for i in range(4):
        block = order[jnp.minimum(first + i, NBLK - 1)]
        column = jnp.sum(jnp.where(which == block, scale, 0.0), axis=1, keepdims=True)
        columns = jnp.where(place == i, column, columns)
    spread[...] = columns
    shape = (48, GROUPS * 32)
    col = iota(shape, 1)
    stored = ((21 * ((col >> 5) ^ FAR)) >> 3) + (col & 3) == iota(shape, 0)
    shape = (48, 48)
    row, col = iota(shape, 0), iota(shape, 1)
    moved = jnp.zeros(shape, F32)
    for s in range(NBLK):
        moved = jnp.where((col == s) & (row == order[s]), 1.0, moved)
    pick[...] = jnp.dot(
        moved.astype(BF16), stored.astype(F32).astype(BF16), preferred_element_type=F32
    ).astype(BF16)
    position = length[core].astype(F32)
    angle = position * freq[...]
    table[0:1, :] = jnp.cos(angle)
    table[1:2, :] = jnp.sin(angle)
    table[2:8, :] = jnp.full((6, PAIR), position, F32)
    for transfer in transfers[4:]:
        transfer.wait()


def project(x, weight, spread, keep, send, wide, blocks):
    group, core = lax.axis_index("group"), lax.axis_index("mp") % 2
    shift = (21 * group) % 8 * 16
    total = jnp.zeros((2 * GROUPS, COLS), F32)
    for i in range(spread.shape[0]):
        part = slice(i * BLK, (i + 1) * BLK)
        dot = lax.dot_general(
            x[:, part], weight[:, part], (((1,), (1,)), ((), ())), preferred_element_type=F32
        )
        total += dot * spread[i : i + 1, :]
    wide[...] = jnp.zeros_like(wide)
    for i in range(3):
        end = min(COLS, (i + 1) * LANES)
        wide[:, i * LANES : end] = total[:, i * LANES : end]
    turned = pltpu.roll(wide[...], shift, 1)
    for i in range(4):
        part = slice(i * LANES, (i + 1) * LANES)
        blocks[i] = turned[:, part]
        keep[:, part] = blocks[i, pl.ds(core, GROUPS, stride=2), :]
        send[:, part] = blocks[i, pl.ds(1 - core, GROUPS, stride=2), :]


def pair_sum(keep, other, out, rows):
    for i in range(4):
        part = slice(i * LANES, (i + 1) * LANES)
        total = keep[:, part] + other[:, part]
        rows[pl.ds(i, GROUPS, stride=8), :] = total
        rows[pl.ds(i + 4, GROUPS, stride=8), :] = total
    out[...] = copies(rows[...])


def attend(table, pick, parts, mine, cache, other, out, keys, values, sems, logical, halves, rows):
    device = lax.axis_index("mp")
    core, chip = device % 2, device // 2
    transfers = []
    moves = (
        (other.at[core, :, pl.ds(0, PAIR)], keys),
        (cache.at[core, pl.ds(EARLY, CTX - EARLY), pl.ds(PAIR, PAIR)], values.at[pl.ds(0, CTX - EARLY), :]),
        (other.at[core, :, pl.ds(PAIR, PAIR)], values.at[pl.ds(CTX - EARLY, CTX), :]),
    )
    for i, (source, target) in enumerate(moves):
        copy = pltpu.make_async_copy(source, target, sems.at[i])
        copy.start()
        transfers.append(copy)

    logical[...] = jnp.dot(pick[...], parts[...], preferred_element_type=F32)
    pairs = jnp.concatenate([logical[pl.ds(t, 16, stride=3), :] for t in range(3)], axis=1)

    shape = (16, PAIR)
    row, lane = iota(shape, 0), iota(shape, 1)
    cosine, sine = table[0:1, :], table[1:2, :]
    position = table[2:3, :1].astype(jnp.int32)
    partner = jnp.where(lane % HD < HALF, -pltpu.roll(pairs, PAIR - HALF, 1), pltpu.roll(pairs, HALF, 1))
    turned = jnp.where(row == 13, pairs, pairs * cosine + partner * sine)
    turned = turned.astype(BF16).astype(F32)
    own_head = (row < 6) == (lane < HD)
    used = own_head & (row < 12)
    query = jnp.concatenate(
        [jnp.where(used, turned, 0.0), jnp.where(used, pltpu.roll(turned, HD, 1), 0.0)], axis=0
    )
    factor = HD ** (-0.5)
    new = jnp.sum(query * turned[12:13, :], axis=1, keepdims=True) * factor
    new = jnp.where(chip == 0, new, NEG)
    query = query.astype(BF16)

    top = new
    scores = []
    for half, source in enumerate((mine, keys)):
        if half:
            transfers[0].wait()
        base = (device, device + 1 - 2 * core)[half] * CTX
        score = lax.dot_general(
            query, source[:CTX, :], (((1,), (1,)), ((), ())), preferred_element_type=F32
        )
        valid = iota(score.shape, 1) < position - base
        score = jnp.where(valid, score * factor, NEG)
        top = jnp.maximum(top, jnp.max(score, axis=1, keepdims=True))
        scores.append((score, valid))
    own = jnp.where(chip == 0, jnp.exp(new - top), 0.0)
    total = own
    value = own * turned[13:14, :]
    transfers[1].wait()
    transfers[2].wait()
    weights = []
    for score, valid in scores:
        weight = jnp.where(valid, jnp.exp(score - top), 0.0)
        total += jnp.sum(weight, axis=1, keepdims=True)
        weights.append(weight.astype(BF16))
    value += jnp.dot(weights[0][:, :EARLY], mine[CTX:, :], preferred_element_type=F32)
    value += jnp.dot(
        weights[0][:, EARLY:], values[: CTX - EARLY, :], preferred_element_type=F32
    )
    value += jnp.dot(weights[1], values[CTX - EARLY :, :], preferred_element_type=F32)
    some = total > 0.0
    safe = jnp.where(some, total, 1.0)
    value = value / safe
    level = jnp.where(some, top + jnp.log(safe), NEG)

    merged = jnp.where(own_head, value[:16], pltpu.roll(value[16:], HD, 1))
    low = iota((16, 1), 0) < 6
    even = jnp.where(low, level[:16], level[16:])
    odd = jnp.where(low, level[16:], level[:16])
    lane = iota((16, LANES), 1)
    for w in range(4):
        data = merged if w == 0 else pltpu.roll(merged, PAIR - HALF * w, 1)
        level = even if w < 2 else odd
        high = level.astype(BF16).astype(F32)
        middle = (level - high).astype(BF16).astype(F32)
        tail = level - high - middle
        terms = jnp.where(lane == HALF, high, jnp.where(lane == HALF + 1, middle, jnp.where(lane == HALF + 2, tail, 0.0)))
        halves[pl.ds(w, 16, stride=4), :] = jnp.where(lane < HALF, data[:, :LANES], terms)
    rows[...] = jnp.zeros_like(rows)
    for u in range(3):
        data = halves[pl.ds(u, GROUPS, stride=3), :]
        rows[pl.ds(u, GROUPS, stride=8), :] = data
        rows[pl.ds(u + 4, GROUPS, stride=8), :] = data
    data = rows[...].reshape(GROUPS, 8, LANES)
    out[...] = copies(jnp.concatenate([data[p ^ FAR] for p in range(GROUPS)], axis=0))


def merge(parts, out, rows):
    shape = (LANES, LANES)
    term = iota(shape, 0)
    pick = ((term >= HALF) & (term < HALF + 3)).astype(F32).astype(BF16)
    data = parts[...]
    shape = (GROUPS, 4, 8, LANES)
    level = jnp.dot(data, pick, preferred_element_type=F32).reshape(shape)
    data = data.astype(F32).reshape(shape)

    def both(fn, x):
        x = x.reshape(GROUPS * 8, LANES)
        rows[...] = x
        turned = jnp.concatenate([rows[4:, :], rows[:4, :]], axis=0)
        sub = iota(x.shape, 0) % 8
        back = jnp.concatenate([rows[-4:, :], rows[:-4, :]], axis=0)
        return fn(x, jnp.where(sub < 4, turned, back))

    top = both(jnp.maximum, jnp.max(level, axis=1)).reshape(GROUPS, 1, 8, LANES)
    weight = jnp.exp(level - top)
    total = both(jnp.add, jnp.sum(weight, axis=1))
    value = both(jnp.add, jnp.sum(weight * data, axis=1))
    value = jnp.where(iota(value.shape, 1) < HALF, value / total, 0.0)
    rows[...] = value
    for u in range(3):
        out[u] = rows[pl.ds(u, GROUPS, stride=8), :].astype(BF16)


def project_out(mine, other, values, scales, out, rows):
    first = (9 * lax.axis_index("group")) // 4
    group = lax.axis_index("group")
    shift = (9 * group) % 4 * 32
    lane = iota((2 * GROUPS, LANES), 1)
    width = values.shape[1]
    total = jnp.zeros((3 * 2 * GROUPS, width), F32)
    for u in range(3):
        data = jnp.concatenate([mine[u], other[u]], axis=0)
        block = (lane + shift + HALF * u) // BLK
        data = jnp.concatenate([jnp.where(block == i, data, jnp.zeros_like(data)) for i in range(3)], axis=0)
        total += jnp.dot(
            data[:, :HALF], values[HALF * u : HALF * (u + 1), :], preferred_element_type=F32
        )
    result = jnp.zeros((2 * GROUPS, width), F32)
    scale = scales[...]
    for i in range(3):
        column = jnp.sum(jnp.where(iota(scale.shape, 1) == first + i, scale, 0.0), axis=1, keepdims=True)
        wide = [jnp.broadcast_to(column[j : j + 1, :], (1, BLK)) for j in range(scale.shape[0])]
        result += total[2 * GROUPS * i : 2 * GROUPS * (i + 1)] * jnp.concatenate(wide, axis=1)
    rows[:, 0, :] = result[:GROUPS]
    rows[:, 1, :] = result[GROUPS:]
    out[...] = rows[...].astype(BF16)


def finish(parts, out):
    total = jnp.sum(parts[...].astype(F32), axis=0)
    swapped = jnp.concatenate([total[1:2], total[0:1]], axis=0)
    out[...] = jnp.where(lax.axis_index("mp") % 2 == 0, total, swapped).astype(BF16)


def call(kernel, shapes, in_specs, scratch, args, limit=16):
    single = not isinstance(shapes, (list, tuple))
    args = [
        pltpu.with_memory_space_constraint(arg, pltpu.HBM) if spec is HBM else arg
        for arg, spec in zip(args, in_specs)
    ]
    return pl.pallas_call(
        kernel,
        out_shape=shapes,
        in_specs=in_specs,
        out_specs=VMEM if single else [VMEM] * len(shapes),
        scratch_shapes=scratch,
        compiler_params=pltpu.CompilerParams(vmem_limit_bytes=limit * 1024 * 1024),
    )(*args)


def local(
    activations, qkv_values, qkv_scales, block_order, out_values, out_scales, kv_cache, cache_len
):
    both = ("group", "mp")
    width = activations.shape[1]
    swap = [(i, i ^ 1) for i in range(2 * CHIPS)]
    same_core = [
        [(g ^ FAR) * 2 * CHIPS + 2 * (k ^ FAR_CHIP) + core for g in range(GROUPS) for k in range(CHIPS)]
        for core in range(2)
    ]
    groups = [[g ^ FAR for g in range(GROUPS)]]

    def exchange(rows):
        chunks = rows.reshape(GROUPS * CHIPS, 4, LANES)
        chunks = lax.all_to_all(chunks, both, 0, 0, tiled=True, axis_index_groups=same_core)
        return chunks.reshape(GROUPS * 32, LANES)

    cache_other = lax.ppermute(kv_cache, "mp", swap)
    x = jnp.broadcast_to(activations[None], (GROUPS,) + activations.shape)
    x = lax.all_to_all(x, "group", 0, 0, tiled=True, axis_index_groups=groups).reshape(2 * GROUPS, width)
    lanes = np.arange(PAIR) % HALF
    freq = (10000.0 ** (-lanes / HALF)).astype(np.float32)[None, :]
    weight, spread, pick, table, keys_mine = call(
        prepare,
        [
            jax.ShapeDtypeStruct((COLS, width), BF16),
            jax.ShapeDtypeStruct((width // BLK, COLS), F32),
            jax.ShapeDtypeStruct((48, GROUPS * 32), BF16),
            jax.ShapeDtypeStruct((8, PAIR), F32),
            jax.ShapeDtypeStruct((CTX + EARLY, PAIR), BF16),
        ],
        [HBM] * 6,
        [
            pltpu.SMEM(block_order.shape, jnp.int32),
            pltpu.SMEM(cache_len.shape, jnp.int32),
            pltpu.VMEM(freq.shape, F32),
            pltpu.VMEM(qkv_scales.shape, F32),
            pltpu.SemaphoreType.DMA((7,)),
        ],
        (block_order, cache_len, jnp.asarray(freq), qkv_values.T, qkv_scales, kv_cache),
    )
    keep, send = call(
        project,
        [jax.ShapeDtypeStruct((GROUPS, 4 * LANES), F32)] * 2,
        [VMEM, VMEM, VMEM],
        [pltpu.VMEM((2 * GROUPS, 4 * LANES), F32), pltpu.VMEM((4, 2 * GROUPS, LANES), F32)],
        (x, weight, spread),
    )
    rows_type = jax.ShapeDtypeStruct((GROUPS * 32, LANES), BF16)
    rows_scratch = pltpu.VMEM((GROUPS * 8, LANES), F32)
    parts = call(
        pair_sum, rows_type, [VMEM, VMEM], [rows_scratch], (keep, lax.ppermute(send, "mp", swap))
    )
    parts = exchange(parts)
    parts = call(
        attend,
        rows_type,
        [VMEM, VMEM, VMEM, VMEM, HBM, HBM],
        [
            pltpu.VMEM((CTX, PAIR), BF16),
            pltpu.VMEM((2 * CTX - EARLY, PAIR), BF16),
            pltpu.SemaphoreType.DMA((3,)),
            pltpu.VMEM((48, LANES), F32),
            pltpu.VMEM((64, LANES), F32),
            rows_scratch,
        ],
        (table, pick, parts, keys_mine, kv_cache, cache_other),
    )
    parts = exchange(parts)
    heads = call(
        merge, jax.ShapeDtypeStruct((3, GROUPS, LANES), BF16), [VMEM], [rows_scratch], (parts,)
    )
    result = call(
        project_out,
        jax.ShapeDtypeStruct((GROUPS, 2, width), BF16),
        [VMEM] * 4,
        [pltpu.VMEM((GROUPS, 2, width), F32)],
        (heads, lax.ppermute(heads, "mp", swap), out_values, out_scales.T),
    )
    result = lax.all_to_all(result, "group", 0, 0, tiled=True, axis_index_groups=groups)
    return call(finish, jax.ShapeDtypeStruct((2, width), BF16), [VMEM], [], (result,))


def solution(mesh):
    placed = (
        P("group", "mp"),
        P("mp", "group"),
        P("mp", None),
        P(),
        P("group", "mp"),
        P(None, "mp"),
        P("group", "mp", None),
        P("group"),
    )
    return jax.shard_map(
        local, mesh=mesh, in_specs=placed, out_specs=P("group", "mp"), check_vma=False
    )
```

```python
import jax
import jax.numpy as jnp
import numpy as np
from jax import lax
from jax.experimental import pallas as pl
from jax.experimental.pallas import tpu as pltpu
from jax.sharding import PartitionSpec as P

HD = 192
BLK = 128
LANES = 128
PAIR = 2 * HD
HALF = HD // 2
NBLK = 42
COLS = 336
GROUPS = 16
CHIPS = 8
FAR = 10
FAR_CHIP = 4
CTX = 2048
EARLY = 1024
NEG = -1e30
F32 = jnp.float32
BF16 = jnp.bfloat16

VMEM = pl.BlockSpec(memory_space=pltpu.VMEM)
SMEM = pl.BlockSpec(memory_space=pltpu.SMEM)
HBM = pl.BlockSpec(memory_space=pltpu.HBM)


def iota(shape, dim):
    return lax.broadcasted_iota(jnp.int32, shape, dim)


def copies(rows):
    spread = jnp.broadcast_to(rows.reshape(GROUPS, 1, 8, LANES), (GROUPS, 4, 8, LANES))
    return spread.reshape(GROUPS * 32, LANES).astype(BF16)


def prepare(
    order_in, length_in, freq_in, values, scales_in, cache,
    weight, spread, pick, table, mine,
    order, length, freq, scales, sems,
):
    group, core = lax.axis_index("group"), lax.axis_index("mp") % 2
    pairs = (
        (order_in, order),
        (length_in, length),
        (scales_in, scales),
        (freq_in, freq),
        (values, weight),
        (cache.at[core, :, pl.ds(0, PAIR)], mine.at[pl.ds(0, CTX), :]),
        (cache.at[core, pl.ds(0, EARLY), pl.ds(PAIR, PAIR)], mine.at[pl.ds(CTX, EARLY), :]),
    )
    transfers = [
        pltpu.make_async_copy(source, target, sems.at[i]) for i, (source, target) in enumerate(pairs)
    ]
    for transfer in transfers:
        transfer.start()
    for transfer in transfers[:4]:
        transfer.wait()
    first = (21 * group) // 8
    shift = (21 * group - 8 * first) * 16
    scale = scales[...]
    rows = scale.shape[0]
    which = iota((rows, NBLK), 1)
    place = (iota((rows, COLS), 1) + shift) // BLK
    columns = jnp.zeros((rows, COLS), F32)
    for i in range(4):
        block = order[jnp.minimum(first + i, NBLK - 1)]
        column = jnp.sum(jnp.where(which == block, scale, 0.0), axis=1, keepdims=True)
        columns = jnp.where(place == i, column, columns)
    spread[...] = columns
    shape = (48, GROUPS * 32)
    col = iota(shape, 1)
    stored = ((21 * ((col >> 5) ^ FAR)) >> 3) + (col & 3) == iota(shape, 0)
    shape = (48, 48)
    row, col = iota(shape, 0), iota(shape, 1)
    moved = jnp.zeros(shape, F32)
    for s in range(NBLK):
        moved = jnp.where((col == s) & (row == order[s]), 1.0, moved)
    pick[...] = jnp.dot(
        moved.astype(BF16), stored.astype(F32).astype(BF16), preferred_element_type=F32
    ).astype(BF16)
    position = length[core].astype(F32)
    angle = position * freq[...]
    table[0:1, :] = jnp.cos(angle)
    table[1:2, :] = jnp.sin(angle)
    table[2:8, :] = jnp.full((6, PAIR), position, F32)
    for transfer in transfers[4:]:
        transfer.wait()


def project(x, weight, spread, keep, send, wide, blocks):
    group, core = lax.axis_index("group"), lax.axis_index("mp") % 2
    shift = (21 * group) % 8 * 16
    total = jnp.zeros((2 * GROUPS, COLS), F32)
    for i in range(spread.shape[0]):
        part = slice(i * BLK, (i + 1) * BLK)
        dot = lax.dot_general(
            x[:, part], weight[:, part], (((1,), (1,)), ((), ())), preferred_element_type=F32
        )
        total += dot * spread[i : i + 1, :]
    wide[...] = jnp.zeros_like(wide)
    for i in range(3):
        end = min(COLS, (i + 1) * LANES)
        wide[:, i * LANES : end] = total[:, i * LANES : end]
    turned = pltpu.roll(wide[...], shift, 1)
    for i in range(4):
        part = slice(i * LANES, (i + 1) * LANES)
        blocks[i] = turned[:, part]
        keep[:, part] = blocks[i, pl.ds(core, GROUPS, stride=2), :]
        send[:, part] = blocks[i, pl.ds(1 - core, GROUPS, stride=2), :]


def pair_sum(keep, other, out, rows):
    for i in range(4):
        part = slice(i * LANES, (i + 1) * LANES)
        total = keep[:, part] + other[:, part]
        rows[pl.ds(i, GROUPS, stride=8), :] = total
        rows[pl.ds(i + 4, GROUPS, stride=8), :] = total
    out[...] = copies(rows[...])


def attend(table, pick, parts, mine, cache, other, out, keys, values, sems, logical, halves, rows):
    device = lax.axis_index("mp")
    core, chip = device % 2, device // 2
    transfers = []
    moves = (
        (other.at[core, :, pl.ds(0, PAIR)], keys),
        (cache.at[core, pl.ds(EARLY, CTX - EARLY), pl.ds(PAIR, PAIR)], values.at[pl.ds(0, CTX - EARLY), :]),
        (other.at[core, :, pl.ds(PAIR, PAIR)], values.at[pl.ds(CTX - EARLY, CTX), :]),
    )
    for i, (source, target) in enumerate(moves):
        copy = pltpu.make_async_copy(source, target, sems.at[i])
        copy.start()
        transfers.append(copy)

    logical[...] = jnp.dot(pick[...], parts[...], preferred_element_type=F32)
    pairs = jnp.concatenate([logical[pl.ds(t, 16, stride=3), :] for t in range(3)], axis=1)

    shape = (16, PAIR)
    row, lane = iota(shape, 0), iota(shape, 1)
    cosine, sine = table[0:1, :], table[1:2, :]
    position = table[2:3, :1].astype(jnp.int32)
    partner = jnp.where(lane % HD < HALF, -pltpu.roll(pairs, PAIR - HALF, 1), pltpu.roll(pairs, HALF, 1))
    turned = jnp.where(row == 13, pairs, pairs * cosine + partner * sine)
    turned = turned.astype(BF16).astype(F32)
    own_head = (row < 6) == (lane < HD)
    used = own_head & (row < 12)
    query = jnp.concatenate(
        [jnp.where(used, turned, 0.0), jnp.where(used, pltpu.roll(turned, HD, 1), 0.0)], axis=0
    )
    factor = HD ** (-0.5)
    new = jnp.sum(query * turned[12:13, :], axis=1, keepdims=True) * factor
    new = jnp.where(chip == 0, new, NEG)
    query = query.astype(BF16)

    top = new
    scores = []
    for half, source in enumerate((mine, keys)):
        if half:
            transfers[0].wait()
        base = (device, device + 1 - 2 * core)[half] * CTX
        score = lax.dot_general(
            query, source[:CTX, :], (((1,), (1,)), ((), ())), preferred_element_type=F32
        )
        valid = iota(score.shape, 1) < position - base
        score = jnp.where(valid, score * factor, NEG)
        top = jnp.maximum(top, jnp.max(score, axis=1, keepdims=True))
        scores.append((score, valid))
    own = jnp.where(chip == 0, jnp.exp(new - top), 0.0)
    total = own
    value = own * turned[13:14, :]
    weights = []
    for score, valid in scores:
        weight = jnp.where(valid, jnp.exp(score - top), 0.0)
        total += jnp.sum(weight, axis=1, keepdims=True)
        weights.append(weight.astype(BF16))
    value += jnp.dot(weights[0][:, :EARLY], mine[CTX:, :], preferred_element_type=F32)
    transfers[1].wait()
    value += jnp.dot(
        weights[0][:, EARLY:], values[: CTX - EARLY, :], preferred_element_type=F32
    )
    transfers[2].wait()
    value += jnp.dot(weights[1], values[CTX - EARLY :, :], preferred_element_type=F32)
    some = total > 0.0
    safe = jnp.where(some, total, 1.0)
    value = value / safe
    level = jnp.where(some, top + jnp.log(safe), NEG)

    merged = jnp.where(own_head, value[:16], pltpu.roll(value[16:], HD, 1))
    low = iota((16, 1), 0) < 6
    even = jnp.where(low, level[:16], level[16:])
    odd = jnp.where(low, level[16:], level[:16])
    lane = iota((16, LANES), 1)
    for w in range(4):
        data = merged if w == 0 else pltpu.roll(merged, PAIR - HALF * w, 1)
        level = even if w < 2 else odd
        high = level.astype(BF16).astype(F32)
        middle = (level - high).astype(BF16).astype(F32)
        tail = level - high - middle
        terms = jnp.where(lane == HALF, high, jnp.where(lane == HALF + 1, middle, jnp.where(lane == HALF + 2, tail, 0.0)))
        halves[pl.ds(w, 16, stride=4), :] = jnp.where(lane < HALF, data[:, :LANES], terms)
    rows[...] = jnp.zeros_like(rows)
    for u in range(3):
        data = halves[pl.ds(u, GROUPS, stride=3), :]
        rows[pl.ds(u, GROUPS, stride=8), :] = data
        rows[pl.ds(u + 4, GROUPS, stride=8), :] = data
    data = rows[...].reshape(GROUPS, 8, LANES)
    out[...] = copies(jnp.concatenate([data[p ^ FAR] for p in range(GROUPS)], axis=0))


def merge(parts, out, rows):
    shape = (LANES, LANES)
    term = iota(shape, 0)
    pick = ((term >= HALF) & (term < HALF + 3)).astype(F32).astype(BF16)
    data = parts[...]
    shape = (GROUPS, 4, 8, LANES)
    level = jnp.dot(data, pick, preferred_element_type=F32).reshape(shape)
    data = data.astype(F32).reshape(shape)

    def both(fn, x):
        x = x.reshape(GROUPS * 8, LANES)
        rows[...] = x
        turned = jnp.concatenate([rows[4:, :], rows[:4, :]], axis=0)
        sub = iota(x.shape, 0) % 8
        back = jnp.concatenate([rows[-4:, :], rows[:-4, :]], axis=0)
        return fn(x, jnp.where(sub < 4, turned, back))

    top = both(jnp.maximum, jnp.max(level, axis=1)).reshape(GROUPS, 1, 8, LANES)
    weight = jnp.exp(level - top)
    total = both(jnp.add, jnp.sum(weight, axis=1))
    value = both(jnp.add, jnp.sum(weight * data, axis=1))
    value = jnp.where(iota(value.shape, 1) < HALF, value / total, 0.0)
    rows[...] = value
    for u in range(3):
        out[u] = rows[pl.ds(u, GROUPS, stride=8), :].astype(BF16)


def project_out(mine, other, values, scales, out, rows):
    first = (9 * lax.axis_index("group")) // 4
    group = lax.axis_index("group")
    shift = (9 * group) % 4 * 32
    lane = iota((2 * GROUPS, LANES), 1)
    width = values.shape[1]
    total = jnp.zeros((3 * 2 * GROUPS, width), F32)
    for u in range(3):
        data = jnp.concatenate([mine[u], other[u]], axis=0)
        block = (lane + shift + HALF * u) // BLK
        data = jnp.concatenate([jnp.where(block == i, data, jnp.zeros_like(data)) for i in range(3)], axis=0)
        total += jnp.dot(
            data[:, :HALF], values[HALF * u : HALF * (u + 1), :], preferred_element_type=F32
        )
    result = jnp.zeros((2 * GROUPS, width), F32)
    scale = scales[...]
    for i in range(3):
        column = jnp.sum(jnp.where(iota(scale.shape, 1) == first + i, scale, 0.0), axis=1, keepdims=True)
        wide = [jnp.broadcast_to(column[j : j + 1, :], (1, BLK)) for j in range(scale.shape[0])]
        result += total[2 * GROUPS * i : 2 * GROUPS * (i + 1)] * jnp.concatenate(wide, axis=1)
    rows[:, 0, :] = result[:GROUPS]
    rows[:, 1, :] = result[GROUPS:]
    out[...] = rows[...].astype(BF16)


def finish(parts, out):
    total = jnp.sum(parts[...].astype(F32), axis=0)
    swapped = jnp.concatenate([total[1:2], total[0:1]], axis=0)
    out[...] = jnp.where(lax.axis_index("mp") % 2 == 0, total, swapped).astype(BF16)


def call(kernel, shapes, in_specs, scratch, args, limit=16):
    single = not isinstance(shapes, (list, tuple))
    args = [
        pltpu.with_memory_space_constraint(arg, pltpu.HBM) if spec is HBM else arg
        for arg, spec in zip(args, in_specs)
    ]
    return pl.pallas_call(
        kernel,
        out_shape=shapes,
        in_specs=in_specs,
        out_specs=VMEM if single else [VMEM] * len(shapes),
        scratch_shapes=scratch,
        compiler_params=pltpu.CompilerParams(vmem_limit_bytes=limit * 1024 * 1024),
    )(*args)


def local(
    activations, qkv_values, qkv_scales, block_order, out_values, out_scales, kv_cache, cache_len
):
    both = ("group", "mp")
    width = activations.shape[1]
    swap = [(i, i ^ 1) for i in range(2 * CHIPS)]
    same_core = [
        [(g ^ FAR) * 2 * CHIPS + 2 * ((CHIPS - k) % CHIPS ^ FAR_CHIP) + core for g in range(GROUPS) for k in range(CHIPS)]
        for core in range(2)
    ]
    groups = [[g ^ FAR for g in range(GROUPS)]]

    def exchange(rows):
        chunks = rows.reshape(GROUPS * CHIPS, 4, LANES)
        chunks = lax.all_to_all(chunks, both, 0, 0, tiled=True, axis_index_groups=same_core)
        return chunks.reshape(GROUPS * 32, LANES)

    cache_other = lax.ppermute(kv_cache, "mp", swap)
    x = jnp.broadcast_to(activations[None], (GROUPS,) + activations.shape)
    x = lax.all_to_all(x, "group", 0, 0, tiled=True, axis_index_groups=groups).reshape(2 * GROUPS, width)
    lanes = np.arange(PAIR) % HALF
    freq = (10000.0 ** (-lanes / HALF)).astype(np.float32)[None, :]
    weight, spread, pick, table, keys_mine = call(
        prepare,
        [
            jax.ShapeDtypeStruct((COLS, width), BF16),
            jax.ShapeDtypeStruct((width // BLK, COLS), F32),
            jax.ShapeDtypeStruct((48, GROUPS * 32), BF16),
            jax.ShapeDtypeStruct((8, PAIR), F32),
            jax.ShapeDtypeStruct((CTX + EARLY, PAIR), BF16),
        ],
        [HBM] * 6,
        [
            pltpu.SMEM(block_order.shape, jnp.int32),
            pltpu.SMEM(cache_len.shape, jnp.int32),
            pltpu.VMEM(freq.shape, F32),
            pltpu.VMEM(qkv_scales.shape, F32),
            pltpu.SemaphoreType.DMA((7,)),
        ],
        (block_order, cache_len, jnp.asarray(freq), qkv_values.T, qkv_scales, kv_cache),
    )
    keep, send = call(
        project,
        [jax.ShapeDtypeStruct((GROUPS, 4 * LANES), F32)] * 2,
        [VMEM, VMEM, VMEM],
        [pltpu.VMEM((2 * GROUPS, 4 * LANES), F32), pltpu.VMEM((4, 2 * GROUPS, LANES), F32)],
        (x, weight, spread),
    )
    rows_type = jax.ShapeDtypeStruct((GROUPS * 32, LANES), BF16)
    rows_scratch = pltpu.VMEM((GROUPS * 8, LANES), F32)
    parts = call(
        pair_sum, rows_type, [VMEM, VMEM], [rows_scratch], (keep, lax.ppermute(send, "mp", swap))
    )
    parts = exchange(parts)
    parts = call(
        attend,
        rows_type,
        [VMEM, VMEM, VMEM, VMEM, HBM, HBM],
        [
            pltpu.VMEM((CTX, PAIR), BF16),
            pltpu.VMEM((2 * CTX - EARLY, PAIR), BF16),
            pltpu.SemaphoreType.DMA((3,)),
            pltpu.VMEM((48, LANES), F32),
            pltpu.VMEM((64, LANES), F32),
            rows_scratch,
        ],
        (table, pick, parts, keys_mine, kv_cache, cache_other),
    )
    parts = exchange(parts)
    heads = call(
        merge, jax.ShapeDtypeStruct((3, GROUPS, LANES), BF16), [VMEM], [rows_scratch], (parts,)
    )
    result = call(
        project_out,
        jax.ShapeDtypeStruct((GROUPS, 2, width), BF16),
        [VMEM] * 4,
        [pltpu.VMEM((GROUPS, 2, width), F32)],
        (heads, lax.ppermute(heads, "mp", swap), out_values, out_scales.T),
    )
    result = lax.all_to_all(result, "group", 0, 0, tiled=True, axis_index_groups=groups)
    return call(finish, jax.ShapeDtypeStruct((2, width), BF16), [VMEM], [], (result,))


def solution(mesh):
    placed = (
        P("group", "mp"),
        P("mp", "group"),
        P("mp", None),
        P(),
        P("group", "mp"),
        P(None, "mp"),
        P("group", "mp", None),
        P("group"),
    )
    return jax.shard_map(
        local, mesh=mesh, in_specs=placed, out_specs=P("group", "mp"), check_vma=False
    )
```
